1024 devices in a mesh: blk: 256 (over x_hi, y, z), mp: 4 (over x_lo, core).
Axes of the slice: x: 4 (x_hi: 2, x_lo: 2; x = x_hi * 2 + x_lo), y: 4, z: 32, core: 2. Of those that a mesh axis runs over, the one named last changes fastest.
Arguments:
- queries: bfloat16 [98304, 2560], P('blk', 'mp'), may hold values from -11 to 11
- keys: bfloat16 [32768, 2560], P('blk', 'mp'), may hold values from -11 to 11
- values: bfloat16 [32768, 2560], P('blk', 'mp'), may hold values from -6 to 6
- out_weight: bfloat16 [2560, 5120], P('mp'), may hold values from -0.125 to 0.125
Outputs:
- mixed: bfloat16 [98304, 5120], P('blk', 'mp')
The draws below stay inside these ranges and needn't reach their ends.
All inputs are finite; a program needn't handle non-finite values.
Results may differ from the reference program's by a relative error of at most 0.018.
Values may be sent and summed in bfloat16 or wider, within the bound.
A program may use at most 32 MiB of HBM per device.

```python
import math
import jax
import jax.numpy as jnp
from jax import lax

D = 5120
H = 20
HS = 128
Q_DEV = 384
KV_DEV = 128
HEAD_FEATURES = 2560
NQ = 98304
VOLUME_TOKENS = 32768
N_MP = 4


def draw_queries(key, part):
    attention_output = jnp.clip(jax.random.normal(jax.random.fold_in(key, 1), (NQ, HEAD_FEATURES), jnp.float32), -6.0, 6.0)
    return attention_output.astype(jnp.bfloat16)


def draw_keys(key, part):
    attention_output = jnp.clip(jax.random.normal(jax.random.fold_in(key, 2), (VOLUME_TOKENS, HEAD_FEATURES), jnp.float32), -6.0, 6.0)
    return attention_output.astype(jnp.bfloat16)


def block_scale(key, extent, split, smallest, high):
    def one(dim, blocks):
        heights = jax.random.uniform(jax.random.fold_in(jax.random.fold_in(key, 6), dim), (blocks,), jnp.float32, smallest / len(split), high / len(split))
        return jnp.repeat(jnp.exp(heights), extent[dim] // blocks).reshape((-1,) + (1,) * (len(extent) - dim - 1))

    factor_of = one(*split[0])
    for cut in split[1:]:
        factor_of = factor_of * one(*cut)
    return factor_of


def noise(stream_key, extent, deviation, limit, pieces=(), kind=jnp.bfloat16):
    loudness = block_scale(stream_key, extent, pieces, -0.22, 0.18) if pieces else 1.0
    result = jax.random.normal(stream_key, extent, jnp.float32) * deviation * loudness
    return jnp.minimum(jnp.maximum(result, -limit), limit).astype(kind)


def setup_inputs(seed: int = 0) -> dict:
    key_list = jax.random.split(jax.random.key(seed), 5)
    queries = draw_queries(jax.random.fold_in(key_list[4], 71), 0)
    keys = draw_keys(jax.random.fold_in(key_list[4], 71), 0)
    values = noise(key_list[2], (VOLUME_TOKENS, HEAD_FEATURES), 1.0, 6.0, ((0, 256), (1, 4)))
    out_weight = noise(key_list[3], (HEAD_FEATURES, D), HEAD_FEATURES ** -0.5, 0.125, ((0, 4),))
    return {"queries": queries, "keys": keys, "values": values, "out_weight": out_weight}


def attend_block(query_rows, key_rows, value_rows):
    score_scale = 1.0 / math.sqrt(HS)
    query_heads = query_rows.astype(jnp.float32).reshape(query_rows.shape[0], H, HS)
    key_heads = key_rows.astype(jnp.float32).reshape(key_rows.shape[0], H, HS)
    value_heads = value_rows.astype(jnp.float32).reshape(value_rows.shape[0], H, HS)
    scores = jnp.einsum('qhd,khd->qhk', query_heads, key_heads) * score_scale
    row_max = lax.optimization_barrier(jnp.max(scores, axis=-1, keepdims=True))
    weights = jnp.exp(scores - row_max)
    total = lax.optimization_barrier(jnp.sum(weights, axis=-1))
    weights_bf = lax.optimization_barrier(weights.astype(jnp.bfloat16)).astype(jnp.float32)
    numerator = jnp.einsum('qhk,khd->qhd', weights_bf, value_heads)
    attended = numerator / total[:, :, None]
    return attended.reshape(query_rows.shape[0], HEAD_FEATURES).astype(jnp.bfloat16)

def projection_rows(attended, out_weight):
    group_width = HEAD_FEATURES // N_MP
    summed = jnp.zeros((attended.shape[0], D), jnp.float32)
    for group in range(N_MP):
        cols = attended[:, group * group_width:(group + 1) * group_width]
        rows_w = out_weight[group * group_width:(group + 1) * group_width, :]
        window_partial_sum = jnp.dot(cols, rows_w, preferred_element_type=jnp.float32)
        summed = summed + lax.optimization_barrier(window_partial_sum.astype(jnp.bfloat16)).astype(jnp.float32)
    return summed.astype(jnp.bfloat16)

def reference(queries, keys, values, out_weight):
    blocks = NQ // Q_DEV
    query_grid = queries.reshape(blocks, Q_DEV, HEAD_FEATURES)
    key_grid = keys.reshape(blocks, KV_DEV, HEAD_FEATURES)
    value_grid = values.reshape(blocks, KV_DEV, HEAD_FEATURES)

    def per_block(which_block):
        nearby = (which_block + jnp.arange(-2, 3, dtype=jnp.int32) + blocks) % blocks
        key_rows = jnp.take(key_grid, nearby, axis=0).reshape(5 * KV_DEV, HEAD_FEATURES)
        value_rows = jnp.take(value_grid, nearby, axis=0).reshape(5 * KV_DEV, HEAD_FEATURES)
        query_rows = lax.dynamic_index_in_dim(query_grid, which_block, 0, keepdims=False)
        return projection_rows(attend_block(query_rows, key_rows, value_rows), out_weight)
    attention_output = lax.map(per_block, jnp.arange(blocks, dtype=jnp.int32))
    return attention_output.reshape(NQ, D)
```

```python
import functools
import math

import jax
import jax.numpy as jnp
from jax import lax
from jax.experimental import pallas as pl
from jax.experimental.pallas import tpu as pltpu
from jax.sharding import PartitionSpec as P

HS = 128
MESH = pl.DeviceIdType.MESH
ROW_TILE = 128


def kernel(
    q_hbm, k_hbm, v_hbm, w_hbm, o_hbm,
    q, kv, w, att, acc, outgoing, incoming, result,
    kv_sem, load_sem, own_send, own_recv, on_send, on_recv,
    w_send, w_recv, att_send, att_recv, part_send, part_recv, out_sem,
):
    heads, _, window_rows, _ = kv.shape
    rows = q.shape[0]
    block = window_rows // 5
    pieces, _, width = outgoing.shape
    share = pieces * width

    blk, mp = lax.axis_index("blk"), lax.axis_index("mp")
    blocks = lax.axis_size("blk")
    ahead = {"blk": lax.rem(blk + 1, blocks)}
    behind = {"blk": lax.rem(blk + blocks - 1, blocks)}
    core = lax.rem(mp, 2)
    sibling = {"mp": mp + 1 - 2 * core}
    across = {"mp": lax.rem(mp + 2, 4)}

    def slot(j):
        return pl.ds(j * block, block)

    def columns_of(device):
        return pl.ds(pl.multiple_of(device * share, 128), share)

    kv_loads = []
    for h in range(heads):
        for side, ref in enumerate((k_hbm, v_hbm)):
            load = pltpu.make_async_copy(
                ref.at[:, pl.ds(h * HS, HS)], kv.at[h, side, slot(2)], kv_sem.at[h, side]
            )
            load.start()
            kv_loads.append(load)
    q_load = pltpu.make_async_copy(q_hbm, q, load_sem.at[0])
    q_load.start()

    for peer in (ahead, behind, sibling, across):
        pl.semaphore_signal(pltpu.get_barrier_semaphore(), inc=1, device_id=peer, device_id_type=MESH)
    pl.semaphore_wait(pltpu.get_barrier_semaphore(), 4)

    def kv_copy(h, source, target, peer, send, recv, way):
        return pltpu.make_async_remote_copy(
            src_ref=kv.at[h, :, slot(source)],
            dst_ref=kv.at[h, :, slot(target)],
            send_sem=send.at[way, h],
            recv_sem=recv.at[way, h],
            device_id=peer,
            device_id_type=MESH,
        )

    own_copies, on_copies = [], []
    for h in range(heads):
        kv_loads[2 * h].wait()
        kv_loads[2 * h + 1].wait()
        up = kv_copy(h, 2, 1, ahead, own_send, own_recv, 0)
        down = kv_copy(h, 2, 3, behind, own_send, own_recv, 1)
        up.start()
        down.start()
        own_copies.append((up, down))

    w_loads, w_copies = [], []
    for part, base in enumerate((lax.rem(mp + 2, 4), mp)):
        load = pltpu.make_async_copy(
            w_hbm.at[:, :, columns_of(base)],
            w.at[:, pl.ds(0, HS), pl.ds(part * share, share)],
            load_sem.at[1 + part],
        )
        load.start()
        w_loads.append(load)
        copy = pltpu.make_async_remote_copy(
            src_ref=w_hbm.at[:, :, columns_of(base + 1 - 2 * core)],
            dst_ref=w.at[:, pl.ds(HS, HS), pl.ds(part * share, share)],
            send_sem=w_send.at[part],
            recv_sem=w_recv.at[part],
            device_id=sibling,
            device_id_type=MESH,
        )
        copy.start()
        w_copies.append(copy)

    for h in range(heads):
        up = kv_copy(h, 1, 0, ahead, on_send, on_recv, 0)
        down = kv_copy(h, 3, 4, behind, on_send, on_recv, 1)
        own_copies[h][0].wait_recv()
        up.start()
        own_copies[h][1].wait_recv()
        down.start()
        on_copies.append((up, down))

    q_load.wait()
    scale = math.log2(math.e) / math.sqrt(HS)

    def attend(h):
        for r in range(0, rows, ROW_TILE):
            size = min(ROW_TILE, rows - r)
            query = q[pl.ds(r, size), pl.ds(h * HS, HS)]
            scores = lax.dot_general(
                query, kv[h, 0], (((1,), (1,)), ((), ())), preferred_element_type=jnp.float32
            )
            top = jnp.max(scores, axis=1, keepdims=True)
            weights = jnp.exp2(scores * scale - top * scale)
            total = jnp.sum(weights, axis=1, keepdims=True)
            numerator = jnp.dot(
                weights.astype(jnp.bfloat16), kv[h, 1], preferred_element_type=jnp.float32
            )
            att[h, pl.ds(r, size), pl.ds(0, HS)] = (numerator * (1.0 / total)).astype(jnp.bfloat16)

    def project(h, piece):
        return jnp.dot(
            att[h],
            w[h, :, pl.ds(pl.multiple_of(piece * width, 128), width)],
            preferred_element_type=jnp.float32,
        )

    def add_head(h):
        @pl.loop(0, 2 * pieces)
        def _(piece):
            if h == 0:
                acc[piece] = project(h, piece)
            else:
                acc[piece] += project(h, piece)

    att_copies = []
    for h in range(heads):
        on_copies[h][0].wait_recv()
        on_copies[h][1].wait_recv()
        attend(h)
        copy = pltpu.make_async_remote_copy(
            src_ref=att.at[h, :, pl.ds(0, HS)],
            dst_ref=att.at[h, :, pl.ds(HS, HS)],
            send_sem=att_send.at[h],
            recv_sem=att_recv.at[h],
            device_id=sibling,
            device_id_type=MESH,
        )
        copy.start()
        att_copies.append(copy)
        if h == 0:
            for load, arriving in zip(w_loads, w_copies):
                load.wait()
                arriving.wait_recv()
        else:
            att_copies[h - 1].wait_recv()
            add_head(h - 1)
    att_copies[heads - 1].wait_recv()

    def part_copy(piece):
        return pltpu.make_async_remote_copy(
            src_ref=outgoing.at[piece],
            dst_ref=incoming.at[piece],
            send_sem=part_send.at[piece],
            recv_sem=part_recv.at[piece],
            device_id=across,
            device_id_type=MESH,
        )

    for piece in range(pieces):
        outgoing[piece] = (acc[piece] + project(heads - 1, piece)).astype(jnp.bfloat16)
        part_copy(piece).start()

    @pl.loop(pieces, 2 * pieces)
    def _(piece):
        acc[piece] += project(heads - 1, piece)

    stores = []
    for piece in range(pieces):
        part_copy(piece).wait_recv()
        result[piece] = (acc[pieces + piece] + incoming[piece].astype(jnp.float32)).astype(jnp.bfloat16)
        store = pltpu.make_async_copy(
            result.at[piece], o_hbm.at[:, pl.ds(piece * width, width)], out_sem.at[piece]
        )
        store.start()
        stores.append(store)

    for up, down in own_copies + on_copies:
        up.wait_send()
        down.wait_send()
    for copy in w_copies + att_copies:
        copy.wait_send()
    for piece in range(pieces):
        part_copy(piece).wait_send()
    for store in stores:
        store.wait()


def on_device(queries, keys, values, out_weight):
    rows, features = queries.shape
    block = keys.shape[0]
    heads = features // HS
    share = out_weight.shape[1] // lax.axis_size("mp")
    pieces = 5 if share % (5 * 128) == 0 else 2
    width = share // pieces
    dma, bf16 = pltpu.SemaphoreType.DMA, jnp.bfloat16
    flops = 2 * rows * (2 * 5 * block * features + features * out_weight.shape[1])
    return pl.pallas_call(
        kernel,
        out_shape=jax.ShapeDtypeStruct((rows, share), bf16),
        in_specs=[pl.BlockSpec(memory_space=pltpu.HBM)] * 4,
        out_specs=pl.BlockSpec(memory_space=pl.ANY),
        scratch_shapes=[
            pltpu.VMEM((rows, features), bf16),
            pltpu.VMEM((heads, 2, 5 * block, HS), bf16),
            pltpu.VMEM((heads, 2 * HS, 2 * share), bf16),
            pltpu.VMEM((heads, rows, 2 * HS), bf16),
            pltpu.VMEM((2 * pieces, rows, width), jnp.float32),
            pltpu.VMEM((pieces, rows, width), bf16),
            pltpu.VMEM((pieces, rows, width), bf16),
            pltpu.VMEM((pieces, rows, width), bf16),
            dma((heads, 2)),
            dma((3,)),
            dma((2, heads)),
            dma((2, heads)),
            dma((2, heads)),
            dma((2, heads)),
            dma((2,)),
            dma((2,)),
            dma((heads,)),
            dma((heads,)),
            dma((pieces,)),
            dma((pieces,)),
            dma((pieces,)),
        ],
        compiler_params=pltpu.CompilerParams(
            collective_id=0, has_side_effects=True, vmem_limit_bytes=48 * 2**20
        ),
        cost_estimate=pl.CostEstimate(
            flops=flops, bytes_accessed=9_000_000, transcendentals=5 * block * rows * heads
        ),
    )(queries, keys, values, out_weight.reshape(heads, HS, out_weight.shape[1]))


def solution(mesh):
    placed = (P("blk", "mp"), P("blk", "mp"), P("blk", "mp"), P("mp", None))
    return jax.shard_map(
        on_device, mesh=mesh, in_specs=placed, out_specs=P("blk", "mp"), check_vma=False
    )
```

```python
import math

import jax
import jax.numpy as jnp
from jax import lax
from jax.experimental import pallas as pl
from jax.experimental.pallas import tpu as pltpu
from jax.sharding import PartitionSpec as P

HS = 128
MESH = pl.DeviceIdType.MESH
ROW_TILE = 128
PIECE = 256
X_HALVES = 2
Y_CHIPS = 4


def kernel(
    q_hbm, k_hbm, v_hbm, w_hbm, o_hbm,
    q, kv, w, att, acc, result,
    kv_sem, load_sem, own_send, own_recv, on_send, on_recv, sib_send, sib_recv,
    wx_send, wx_recv, wy_send, wy_recv, hand_send, hand_recv, att_send, att_recv, out_sem, ready,
):
    heads, _, window_rows, _ = kv.shape
    rows = q.shape[0]
    block = window_rows // 5
    share = acc.shape[1]
    half = share // 2
    piece_width = min(PIECE, share)
    pieces = share // piece_width

    blk, mp = lax.axis_index("blk"), lax.axis_index("mp")
    blocks = lax.axis_size("blk")
    z_chips = blocks // (X_HALVES * Y_CHIPS)
    x_hi, y, z = blk // (blocks // 2), lax.rem(blk // z_chips, Y_CHIPS), lax.rem(blk, z_chips)
    x_lo, core = mp // 2, lax.rem(mp, 2)
    parity = lax.rem(y, 2)

    def device(b, lo, c):
        return {"blk": b, "mp": 2 * lo + c}

    ahead_blk, behind_blk = lax.rem(blk + 1, blocks), lax.rem(blk + blocks - 1, blocks)
    other_blk = lax.rem(blk + blocks // 2, blocks)
    up_blk = blk + (lax.rem(y + 1, Y_CHIPS) - y) * z_chips
    down_blk = blk + (lax.rem(y + Y_CHIPS - 1, Y_CHIPS) - y) * z_chips
    ahead, behind = device(ahead_blk, x_lo, core), device(behind_blk, x_lo, core)
    y_up, y_down = device(up_blk, x_lo, core), device(down_blk, x_lo, core)
    sibling, across = device(blk, x_lo, 1 - core), device(blk, 1 - x_lo, core)

    def mover(b, lo):
        return device(b, lo, 1 - b // (blocks // 2))

    def greeter(b, lo):
        return device(b, lo, b // (blocks // 2))

    moves_weights = core != x_hi

    def slot(j):
        return pl.ds(j * block, block)

    def columns_of(lo, c):
        return pl.ds(pl.multiple_of((2 * lo + c) * share, 128), share)

    kv_loads = []
    for h in range(heads):
        for side, ref in enumerate((k_hbm, v_hbm)):
            load = pltpu.make_async_copy(
                ref.at[:, pl.ds(h * HS, HS)], kv.at[h, side, slot(2)], kv_sem.at[h, side]
            )
            load.start()
            kv_loads.append(load)

    barrier = pltpu.get_barrier_semaphore()

    def greet(*peers):
        for peer in peers:
            pl.semaphore_signal(barrier, inc=1, device_id=peer, device_id_type=MESH)

    greet(greeter(ahead_blk, x_lo), greeter(behind_blk, x_lo), across)

    @pl.when(moves_weights)
    def _():
        greet(mover(other_blk, 1 - x_lo), y_up, y_down, sibling)

    q_load = pltpu.make_async_copy(q_hbm, q, load_sem.at[0])
    q_load.start()
    w_load = pltpu.make_async_copy(
        w_hbm.at[:, :, :, columns_of(x_lo, core)], w.at[:, 0], load_sem.at[1]
    )
    w_load.start()

    pl.semaphore_wait(barrier, jnp.where(moves_weights, 4, 6))

    @pl.when(jnp.logical_not(moves_weights))
    def _():
        pl.semaphore_signal(ready, inc=1, device_id=sibling, device_id_type=MESH)

    def wx_copies(h):
        for chip in range(2):
            for own in range(2):
                target = 1 - core if chip == own else core
                yield pltpu.make_async_remote_copy(
                    src_ref=w_hbm.at[h, parity, :, columns_of(1 - x_lo, target)],
                    dst_ref=w.at[h, 2 + chip if own else 5 - chip, parity],
                    send_sem=wx_send.at[h, chip, own],
                    recv_sem=wx_recv.at[h, chip, own],
                    device_id=mover(other_blk if chip else blk, 1 - x_lo),
                    device_id_type=MESH,
                )

    def wy_copy(h, way):
        piece = (h, pl.ds(2, 4), parity, slice(None), pl.ds(way * half, half))
        return pltpu.make_async_remote_copy(
            src_ref=w.at[piece],
            dst_ref=w.at[piece],
            send_sem=wy_send.at[h, way],
            recv_sem=wy_recv.at[h, way],
            device_id=y_up if way else y_down,
            device_id_type=MESH,
        )

    def hand_over(h):
        return pltpu.make_async_remote_copy(
            src_ref=w.at[h, pl.ds(4, 2)],
            dst_ref=w.at[h, pl.ds(2, 2)],
            send_sem=hand_send.at[h],
            recv_sem=hand_recv.at[h],
            device_id=sibling,
            device_id_type=MESH,
        )

    def send_on_x(h):
        for copy in wx_copies(h):
            copy.start()

    def send_on_y(h):
        for copy in wx_copies(h):
            copy.wait_recv()
        wy_copy(h, 0).start()
        wy_copy(h, 1).start()
        for copy in wx_copies(h):
            copy.wait_send()
        if h + 2 < heads:
            send_on_x(h + 2)

    def move_when(condition, first, last):
        @pl.when(jnp.logical_and(moves_weights, condition))
        def _():
            for h in range(first, last):
                send_on_y(h)

    def give_weights(h):
        @pl.when(moves_weights)
        def _():
            wy_copy(h, 0).wait_recv()
            wy_copy(h, 1).wait_recv()
            hand_over(h).start()

    @pl.when(moves_weights)
    def _():
        for h in range(min(2, heads)):
            send_on_x(h)

    sib_copy = pltpu.make_async_remote_copy(
        src_ref=w_hbm.at[:, :, :, columns_of(x_lo, 1 - core)],
        dst_ref=w.at[:, 1],
        send_sem=sib_send,
        recv_sem=sib_recv,
        device_id=sibling,
        device_id_type=MESH,
    )

    early = min(3, heads)
    move_when(z == 0, 0, early)

    @pl.when(moves_weights)
    def _():
        pl.semaphore_wait(ready, 1)

    def kv_copy(h, source, target, peer, send, recv, way):
        return pltpu.make_async_remote_copy(
            src_ref=kv.at[h, :, slot(source)],
            dst_ref=kv.at[h, :, slot(target)],
            send_sem=send.at[way, h],
            recv_sem=recv.at[way, h],
            device_id=peer,
            device_id_type=MESH,
        )

    own_copies = [
        (
            kv_copy(h, 2, 1, ahead, own_send, own_recv, 0),
            kv_copy(h, 2, 3, behind, own_send, own_recv, 1),
        )
        for h in range(heads)
    ]
    on_copies = [
        (
            kv_copy(h, 1, 0, ahead, on_send, on_recv, 0),
            kv_copy(h, 3, 4, behind, on_send, on_recv, 1),
        )
        for h in range(heads)
    ]

    def send_own(h):
        kv_loads[2 * h].wait()
        kv_loads[2 * h + 1].wait()
        for copy in own_copies[h]:
            copy.start()

    def pass_block(h, way):
        own_copies[h][way].wait_recv()
        on_copies[h][way].start()

    for h in range(heads):
        send_own(h)
    sib_copy.start()

    @pl.when(z <= 1)
    def _():
        for h in range(heads):
            pass_block(h, 1)

    move_when(z == 1, 0, heads - 1)
    for h in range(heads):
        pass_block(h, 0)
        if h % 2 == 1 and early < heads:
            move_when(z == 0, early, early + 1)
            early += 1

    @pl.when(z > 1)
    def _():
        for h in range(heads):
            pass_block(h, 1)

    move_when(z == 0, early, heads)
    move_when(z == 1, heads - 1, heads)
    move_when(z == 2, 0, heads)

    q_load.wait()
    scale = math.log2(math.e) / math.sqrt(HS)

    def attend(h):
        for r in range(0, rows, ROW_TILE):
            size = min(ROW_TILE, rows - r)
            query = q[pl.ds(r, size), pl.ds(h * HS, HS)]
            scores = lax.dot_general(
                kv[h, 0], query, (((1,), (1,)), ((), ())), preferred_element_type=jnp.float32
            )
            top = jnp.max(scores, axis=0, keepdims=True)
            weights = jnp.exp2(scores * scale - top * scale)
            total = jnp.sum(weights, axis=0, keepdims=True)
            numerator = lax.dot_general(
                kv[h, 1],
                weights.astype(jnp.bfloat16),
                (((0,), (0,)), ((), ())),
                preferred_element_type=jnp.float32,
            )
            att[h, 0, pl.ds(r, size), :] = (numerator * (1.0 / total)).T.astype(jnp.bfloat16)

    def att_copy(h, source, target, peer):
        return pltpu.make_async_remote_copy(
            src_ref=att.at[h, source],
            dst_ref=att.at[h, target],
            send_sem=att_send.at[h, target - 1],
            recv_sem=att_recv.at[h, target - 1],
            device_id=peer,
            device_id_type=MESH,
        )

    def to_sibling(h):
        return att_copy(h, 0, 1, sibling)

    def to_across(h):
        return att_copy(h, 0, 2, across)

    def pass_on(h):
        return att_copy(h, 2, 3, sibling)

    def project(h, piece):
        columns = pl.ds(piece * piece_width, piece_width)
        gathered = jnp.concatenate([att[h, s] for s in range(4)], axis=1)
        return jnp.dot(
            gathered,
            w[h, pl.ds(0, 4), :, :, columns].reshape(4 * HS, piece_width),
            preferred_element_type=jnp.float32,
        )

    def await_head(h):
        to_sibling(h).wait_recv()
        pass_on(h).wait_recv()

        @pl.when(jnp.logical_not(moves_weights))
        def _():
            hand_over(h).wait_recv()

    def forward_head(h):
        to_across(h).wait_recv()
        pass_on(h).start()

    def add_head(h):
        await_head(h)
        for piece in range(pieces):
            columns = pl.ds(piece * piece_width, piece_width)
            if h == 0:
                acc[:, columns] = project(h, piece)
            else:
                acc[:, columns] += project(h, piece)

    for h in range(heads):
        move_when(z > 2, h, h + 1)
        on_copies[h][0].wait_recv()
        on_copies[h][1].wait_recv()
        attend(h)
        to_across(h).start()
        to_sibling(h).start()
        if h >= 1:
            forward_head(h - 1)
            give_weights(h - 1)
        if h == 1:
            w_load.wait()
            sib_copy.wait_recv()
        if h >= 2:
            add_head(h - 2)
    forward_head(heads - 1)
    give_weights(heads - 1)
    if heads > 1:
        add_head(heads - 2)
    await_head(heads - 1)
    stores = []
    for piece in range(pieces):
        columns = pl.ds(piece * piece_width, piece_width)
        result[:, columns] = (acc[:, columns] + project(heads - 1, piece)).astype(jnp.bfloat16)
        store = pltpu.make_async_copy(
            result.at[:, columns], o_hbm.at[:, columns], out_sem.at[piece]
        )
        store.start()
        stores.append(store)

    sib_copy.wait_send()
    for h in range(heads):
        for copy in own_copies[h] + on_copies[h]:
            copy.wait_send()
        to_sibling(h).wait_send()
        to_across(h).wait_send()
        pass_on(h).wait_send()

    @pl.when(moves_weights)
    def _():
        for h in range(heads):
            wy_copy(h, 0).wait_send()
            wy_copy(h, 1).wait_send()
            hand_over(h).wait_send()

    for store in stores:
        store.wait()


def on_device(queries, keys, values, out_weight):
    rows, features = queries.shape
    block = keys.shape[0]
    heads = features // HS
    width = out_weight.shape[1]
    share = width // lax.axis_size("mp")
    pieces = share // min(PIECE, share)
    dma, bf16 = pltpu.SemaphoreType.DMA, jnp.bfloat16
    flops = 2 * rows * (2 * 5 * block * features + features * width)
    return pl.pallas_call(
        kernel,
        out_shape=jax.ShapeDtypeStruct((rows, share), bf16),
        in_specs=[pl.BlockSpec(memory_space=pl.ANY)] * 4,
        out_specs=pl.BlockSpec(memory_space=pl.ANY),
        scratch_shapes=[
            pltpu.VMEM((rows, features), bf16),
            pltpu.VMEM((heads, 2, 5 * block, HS), bf16),
            pltpu.VMEM((heads, 6, 2, HS // 2, share), bf16),
            pltpu.VMEM((heads, 4, rows, HS), bf16),
            pltpu.VMEM((rows, share), jnp.float32),
            pltpu.VMEM((rows, share), bf16),
            dma((heads, 2)),
            dma((2,)),
            dma((2, heads)),
            dma((2, heads)),
            dma((2, heads)),
            dma((2, heads)),
            dma,
            dma,
            dma((heads, 2, 2)),
            dma((heads, 2, 2)),
            dma((heads, 2)),
            dma((heads, 2)),
            dma((heads,)),
            dma((heads,)),
            dma((heads, 3)),
            dma((heads, 3)),
            dma((pieces,)),
            pltpu.SemaphoreType.REGULAR,
        ],
        compiler_params=pltpu.CompilerParams(
            collective_id=0, has_side_effects=True, vmem_limit_bytes=63 * 2**20
        ),
        cost_estimate=pl.CostEstimate(
            flops=flops, bytes_accessed=9_000_000, transcendentals=5 * block * rows * heads
        ),
    )(queries, keys, values, out_weight.reshape(heads, 2, HS // 2, width))


def solution(mesh):
    placed = (P("blk", "mp"), P("blk", "mp"), P("blk", "mp"), P("mp", None))
    return jax.shard_map(
        on_device, mesh=mesh, in_specs=placed, out_specs=P("blk", "mp"), check_vma=False
    )
```

```python
import math

import jax
import jax.numpy as jnp
from jax import lax
from jax.experimental import pallas as pl
from jax.experimental.pallas import tpu as pltpu
from jax.sharding import PartitionSpec as P

HS = 128
MESH = pl.DeviceIdType.MESH
ROW_TILE = 128
PIECE = 256
X_HALVES = 2
Y_CHIPS = 4


def kernel(
    q_hbm, k_hbm, v_hbm, w_hbm, o_hbm,
    q, kv, w, att, acc, result,
    kv_sem, load_sem, own_send, own_recv, on_send, on_recv, sib_send, sib_recv,
    wx_send, wx_recv, wy_send, wy_recv, hand_send, hand_recv, att_send, att_recv, out_sem, ready,
):
    heads, _, window_rows, _ = kv.shape
    rows = q.shape[0]
    block = window_rows // 5
    share = acc.shape[1]
    half = share // 2
    piece_width = min(PIECE, share)
    pieces = share // piece_width

    blk, mp = lax.axis_index("blk"), lax.axis_index("mp")
    blocks = lax.axis_size("blk")
    z_chips = blocks // (X_HALVES * Y_CHIPS)
    x_hi, y, z = blk // (blocks // 2), lax.rem(blk // z_chips, Y_CHIPS), lax.rem(blk, z_chips)
    x_lo, core = mp // 2, lax.rem(mp, 2)
    parity = lax.rem(y, 2)

    def device(b, lo, c):
        return {"blk": b, "mp": 2 * lo + c}

    ahead_blk, behind_blk = lax.rem(blk + 1, blocks), lax.rem(blk + blocks - 1, blocks)
    other_blk = lax.rem(blk + blocks // 2, blocks)
    up_blk = blk + (lax.rem(y + 1, Y_CHIPS) - y) * z_chips
    down_blk = blk + (lax.rem(y + Y_CHIPS - 1, Y_CHIPS) - y) * z_chips
    ahead, behind = device(ahead_blk, x_lo, core), device(behind_blk, x_lo, core)
    y_up, y_down = device(up_blk, x_lo, core), device(down_blk, x_lo, core)
    sibling, across = device(blk, x_lo, 1 - core), device(blk, 1 - x_lo, core)

    def mover(b, lo):
        return device(b, lo, 1 - b // (blocks // 2))

    def greeter(b, lo):
        return device(b, lo, b // (blocks // 2))

    moves_weights = core != x_hi

    def slot(j):
        return pl.ds(j * block, block)

    def columns_of(lo, c):
        return pl.ds(pl.multiple_of((2 * lo + c) * share, 128), share)

    kv_loads = []
    for h in range(heads):
        for side, ref in enumerate((k_hbm, v_hbm)):
            load = pltpu.make_async_copy(
                ref.at[:, pl.ds(h * HS, HS)], kv.at[h, side, slot(2)], kv_sem.at[h, side]
            )
            load.start()
            kv_loads.append(load)

    barrier = pltpu.get_barrier_semaphore()

    def greet(*peers):
        for peer in peers:
            pl.semaphore_signal(barrier, inc=1, device_id=peer, device_id_type=MESH)

    greet(greeter(ahead_blk, x_lo), greeter(behind_blk, x_lo), across)

    @pl.when(moves_weights)
    def _():
        greet(mover(other_blk, 1 - x_lo), y_up, y_down, sibling)

    q_load = pltpu.make_async_copy(q_hbm, q, load_sem.at[0])
    q_load.start()
    w_load = pltpu.make_async_copy(
        w_hbm.at[:, :, :, columns_of(x_lo, core)], w.at[:, 0], load_sem.at[1]
    )
    w_load.start()

    pl.semaphore_wait(barrier, jnp.where(moves_weights, 4, 6))

    @pl.when(jnp.logical_not(moves_weights))
    def _():
        pl.semaphore_signal(ready, inc=1, device_id=sibling, device_id_type=MESH)

    def wx_copies(h):
        for chip in range(2):
            for own in range(2):
                target = 1 - core if chip == own else core
                yield pltpu.make_async_remote_copy(
                    src_ref=w_hbm.at[h, parity, :, columns_of(1 - x_lo, target)],
                    dst_ref=w.at[h, 2 + chip if own else 5 - chip, parity],
                    send_sem=wx_send.at[h, chip, own],
                    recv_sem=wx_recv.at[h, chip, own],
                    device_id=mover(other_blk if chip else blk, 1 - x_lo),
                    device_id_type=MESH,
                )

    def wy_copy(h, way):
        piece = (h, pl.ds(2, 4), parity, slice(None), pl.ds(way * half, half))
        return pltpu.make_async_remote_copy(
            src_ref=w.at[piece],
            dst_ref=w.at[piece],
            send_sem=wy_send.at[h, way],
            recv_sem=wy_recv.at[h, way],
            device_id=y_up if way else y_down,
            device_id_type=MESH,
        )

    def hand_over(h):
        return pltpu.make_async_remote_copy(
            src_ref=w.at[h, pl.ds(4, 2)],
            dst_ref=w.at[h, pl.ds(2, 2)],
            send_sem=hand_send.at[h],
            recv_sem=hand_recv.at[h],
            device_id=sibling,
            device_id_type=MESH,
        )

    def send_on_x(h):
        for copy in wx_copies(h):
            copy.start()

    def send_on_y(h):
        for copy in wx_copies(h):
            copy.wait_recv()
        wy_copy(h, 0).start()
        wy_copy(h, 1).start()
        for copy in wx_copies(h):
            copy.wait_send()
        if h + 2 < heads:
            send_on_x(h + 2)

    def move_when(condition, first, last):
        @pl.when(jnp.logical_and(moves_weights, condition))
        def _():
            for h in range(first, last):
                send_on_y(h)

    def give_weights(h):
        @pl.when(moves_weights)
        def _():
            wy_copy(h, 0).wait_recv()
            wy_copy(h, 1).wait_recv()
            hand_over(h).start()

    @pl.when(moves_weights)
    def _():
        for h in range(min(2, heads)):
            send_on_x(h)

    sib_copy = pltpu.make_async_remote_copy(
        src_ref=w_hbm.at[:, :, :, columns_of(x_lo, 1 - core)],
        dst_ref=w.at[:, 1],
        send_sem=sib_send,
        recv_sem=sib_recv,
        device_id=sibling,
        device_id_type=MESH,
    )

    early = min(3, heads)
    late = jnp.logical_and(z >= max(z_chips - 2, 3), y > 0)
    move_when(z == 0, 0, early)

    @pl.when(moves_weights)
    def _():
        pl.semaphore_wait(ready, 1)

    def kv_copy(h, source, target, peer, send, recv, way):
        return pltpu.make_async_remote_copy(
            src_ref=kv.at[h, :, slot(source)],
            dst_ref=kv.at[h, :, slot(target)],
            send_sem=send.at[way, h],
            recv_sem=recv.at[way, h],
            device_id=peer,
            device_id_type=MESH,
        )

    own_copies = [
        (
            kv_copy(h, 2, 1, ahead, own_send, own_recv, 0),
            kv_copy(h, 2, 3, behind, own_send, own_recv, 1),
        )
        for h in range(heads)
    ]
    on_copies = [
        (
            kv_copy(h, 1, 0, ahead, on_send, on_recv, 0),
            kv_copy(h, 3, 4, behind, on_send, on_recv, 1),
        )
        for h in range(heads)
    ]

    def send_own(h):
        kv_loads[2 * h].wait()
        kv_loads[2 * h + 1].wait()
        for copy in own_copies[h]:
            copy.start()

    def pass_block(h, way):
        own_copies[h][way].wait_recv()
        on_copies[h][way].start()

    for h in range(heads):
        send_own(h)
    sib_copy.start()

    @pl.when(z <= 1)
    def _():
        for h in range(heads):
            pass_block(h, 1)

    move_when(z == 1, 0, heads - 1)
    for h in range(heads):
        pass_block(h, 0)
        if h % 2 == 1 and early < heads:
            move_when(z == 0, early, early + 1)
            early += 1

    move_when(late, 0, 2)

    @pl.when(z > 1)
    def _():
        for h in range(heads):
            pass_block(h, 1)

    move_when(z == 0, early, heads)
    move_when(z == 1, heads - 1, heads)
    move_when(z == 2, 0, heads)
    move_when(late, 2, heads)

    q_load.wait()
    scale = math.log2(math.e) / math.sqrt(HS)

    def attend(h):
        for r in range(0, rows, ROW_TILE):
            size = min(ROW_TILE, rows - r)
            query = q[pl.ds(r, size), pl.ds(h * HS, HS)]
            scores = lax.dot_general(
                kv[h, 0], query, (((1,), (1,)), ((), ())), preferred_element_type=jnp.float32
            )
            top = jnp.max(scores, axis=0, keepdims=True)
            weights = jnp.exp2(scores * scale - top * scale)
            total = jnp.sum(weights, axis=0, keepdims=True)
            numerator = lax.dot_general(
                kv[h, 1],
                weights.astype(jnp.bfloat16),
                (((0,), (0,)), ((), ())),
                preferred_element_type=jnp.float32,
            )
            att[h, 0, pl.ds(r, size), :] = (numerator * (1.0 / total)).T.astype(jnp.bfloat16)

    def att_copy(h, source, target, peer):
        return pltpu.make_async_remote_copy(
            src_ref=att.at[h, source],
            dst_ref=att.at[h, target],
            send_sem=att_send.at[h, target - 1],
            recv_sem=att_recv.at[h, target - 1],
            device_id=peer,
            device_id_type=MESH,
        )

    def to_sibling(h):
        return att_copy(h, 0, 1, sibling)

    def to_across(h):
        return att_copy(h, 0, 2, across)

    def pass_on(h):
        return att_copy(h, 2, 3, sibling)

    def project(h, piece):
        columns = pl.ds(piece * piece_width, piece_width)
        gathered = jnp.concatenate([att[h, s] for s in range(4)], axis=1)
        return jnp.dot(
            gathered,
            w[h, pl.ds(0, 4), :, :, columns].reshape(4 * HS, piece_width),
            preferred_element_type=jnp.float32,
        )

    def await_head(h):
        to_sibling(h).wait_recv()
        pass_on(h).wait_recv()

        @pl.when(jnp.logical_not(moves_weights))
        def _():
            hand_over(h).wait_recv()

    def forward_head(h):
        to_across(h).wait_recv()
        pass_on(h).start()

    def add_head(h):
        await_head(h)
        for piece in range(pieces):
            columns = pl.ds(piece * piece_width, piece_width)
            if h == 0:
                acc[:, columns] = project(h, piece)
            else:
                acc[:, columns] += project(h, piece)

    for h in range(heads):
        move_when(jnp.logical_and(z > 2, jnp.logical_not(late)), h, h + 1)
        on_copies[h][0].wait_recv()
        on_copies[h][1].wait_recv()
        attend(h)
        to_across(h).start()
        to_sibling(h).start()
        if h == min(2, heads - 1):
            w_load.wait()
            sib_copy.wait_recv()
        if h >= 2:
            forward_head(h - 2)
            give_weights(h - 2)
        if h >= 3:
            add_head(h - 3)
    for h in range(max(heads - 2, 0), heads):
        forward_head(h)
        give_weights(h)
        if h >= 1:
            add_head(h - 1)
    await_head(heads - 1)
    stores = []
    for piece in range(pieces):
        columns = pl.ds(piece * piece_width, piece_width)
        result[:, columns] = (acc[:, columns] + project(heads - 1, piece)).astype(jnp.bfloat16)
        store = pltpu.make_async_copy(
            result.at[:, columns], o_hbm.at[:, columns], out_sem.at[piece]
        )
        store.start()
        stores.append(store)

    sib_copy.wait_send()
    for h in range(heads):
        for copy in own_copies[h] + on_copies[h]:
            copy.wait_send()
        to_sibling(h).wait_send()
        to_across(h).wait_send()
        pass_on(h).wait_send()

    @pl.when(moves_weights)
    def _():
        for h in range(heads):
            wy_copy(h, 0).wait_send()
            wy_copy(h, 1).wait_send()
            hand_over(h).wait_send()

    for store in stores:
        store.wait()


def on_device(queries, keys, values, out_weight):
    rows, features = queries.shape
    block = keys.shape[0]
    heads = features // HS
    width = out_weight.shape[1]
    share = width // lax.axis_size("mp")
    pieces = share // min(PIECE, share)
    dma, bf16 = pltpu.SemaphoreType.DMA, jnp.bfloat16
    flops = 2 * rows * (2 * 5 * block * features + features * width)
    return pl.pallas_call(
        kernel,
        out_shape=jax.ShapeDtypeStruct((rows, share), bf16),
        in_specs=[pl.BlockSpec(memory_space=pl.ANY)] * 4,
        out_specs=pl.BlockSpec(memory_space=pl.ANY),
        scratch_shapes=[
            pltpu.VMEM((rows, features), bf16),
            pltpu.VMEM((heads, 2, 5 * block, HS), bf16),
            pltpu.VMEM((heads, 6, 2, HS // 2, share), bf16),
            pltpu.VMEM((heads, 4, rows, HS), bf16),
            pltpu.VMEM((rows, share), jnp.float32),
            pltpu.VMEM((rows, share), bf16),
            dma((heads, 2)),
            dma((2,)),
            dma((2, heads)),
            dma((2, heads)),
            dma((2, heads)),
            dma((2, heads)),
            dma,
            dma,
            dma((heads, 2, 2)),
            dma((heads, 2, 2)),
            dma((heads, 2)),
            dma((heads, 2)),
            dma((heads,)),
            dma((heads,)),
            dma((heads, 3)),
            dma((heads, 3)),
            dma((pieces,)),
            pltpu.SemaphoreType.REGULAR,
        ],
        compiler_params=pltpu.CompilerParams(
            collective_id=0, has_side_effects=True, vmem_limit_bytes=63 * 2**20
        ),
        cost_estimate=pl.CostEstimate(
            flops=flops, bytes_accessed=9_000_000, transcendentals=5 * block * rows * heads
        ),
    )(queries, keys, values, out_weight.reshape(heads, 2, HS // 2, width))


def solution(mesh):
    placed = (P("blk", "mp"), P("blk", "mp"), P("blk", "mp"), P("mp", None))
    return jax.shard_map(
        on_device, mesh=mesh, in_specs=placed, out_specs=P("blk", "mp"), check_vma=False
    )
```
